32 devices in a mesh: ta: 2 (over y), gx: 4 (over x, core), yz: 4 (over z).
Axes of the slice: x: 2, y: 2, z: 4, core: 2. Of those that a mesh axis runs over, the one named last changes fastest.
Arguments:
- vectors: bfloat16 [2, 3, 32, 32, 64, 128], P(None, None, 'gx', 'yz', 'ta'), parts along dimension 4, may hold values from -6 to 6
- gauge_x: float32 [2, 3, 3, 32, 32, 64], P(None, None, None, 'gx', 'yz', 'ta'), parts along dimension 5, may hold values from -6 to 6
- gauge_y: float32 [2, 3, 3, 32, 32, 64], P(None, None, None, 'gx', 'yz', 'ta'), parts along dimension 5, may hold values from -6 to 6
Outputs:
- elementals: float32 [4, 2, 128, 128], P('ta'), parts along dimension 0
The draws below stay inside these ranges and needn't reach their ends.
There are 2 independent parts, one for each index of `ta`. The reference program is written for one: setup_inputs(seed, part) draws one part's arguments, and reference() takes and returns one part's arrays. A program takes and returns all parts, laid end to end along the dimension named above; each array names one. Nothing has to cross between parts.
All inputs are finite; a program needn't handle non-finite values.
Results may differ from the reference program's by a relative error of at most 0.0029.
Values may be sent and summed in bfloat16 or wider, within the bound.
A program may use at most 64 MiB of HBM per device.

```python
import math
import jax
import jax.numpy as jnp

NV = 128
LZ = 32
NX = 32
NY = 32


def block_levels(key, shape, shards, least, top_value):
    def one(dim, parts):
        heights = jax.random.uniform(jax.random.fold_in(jax.random.fold_in(key, 6), dim), (parts,), jnp.float32, least / len(shards), top_value / len(shards))
        return jnp.repeat(jnp.exp(heights), shape[dim] // parts).reshape((-1,) + (1,) * (len(shape) - dim - 1))

    loudness = one(*shards[0])
    for cut in shards[1:]:
        loudness = loudness * one(*cut)
    return loudness


def centred(key, shape, width, most, cuts=(), held_as=jnp.bfloat16):
    drawn = jax.random.normal(key, shape, jnp.float32) * width
    if len(cuts) > 0:
        drawn = block_levels(key, shape, cuts, -0.22, 0.18) * drawn
    return jnp.clip(drawn, min=-most, max=most).astype(held_as)


def setup_inputs(seed: int = 0, part: int = 0) -> dict:
    key_list = jax.random.split(jax.random.key(seed), 4)
    part_splits = jax.random.split(jax.random.fold_in(key_list[3], part), 4)
    return {
        "vectors": centred(part_splits[0], (2, 3, NX, NY, LZ, NV), 1.0, 6.0, ((2, 4), (3, 4))),
        "gauge_x": centred(part_splits[1], (2, 3, 3, NX, NY, LZ), 0.4, 6.0, ((3, 4), (4, 4)), jnp.float32),
        "gauge_y": centred(part_splits[2], (2, 3, 3, NX, NY, LZ), 0.4, 6.0, ((3, 4), (4, 4)), jnp.float32),
    }


def colour_apply(gauge, source_vectors):
    real_parts = []
    imag_parts = []
    for colour in range(3):
        real_running = jnp.zeros(source_vectors.shape[2:], jnp.float32)
        imaginary_running = jnp.zeros(source_vectors.shape[2:], jnp.float32)
        for inner_product in range(3):
            left_real = gauge[0, colour, inner_product][..., None]
            left_imaginary = gauge[1, colour, inner_product][..., None]
            right_real = source_vectors[0, inner_product].astype(jnp.float32)
            right_imaginary = source_vectors[1, inner_product].astype(jnp.float32)
            real_running = real_running + left_real * right_real - left_imaginary * right_imaginary
            imaginary_running = imaginary_running + left_real * right_imaginary + left_imaginary * right_real
        real_parts.append(real_running)
        imag_parts.append(imaginary_running)
    return jnp.stack([jnp.stack(real_parts), jnp.stack(imag_parts)]).astype(jnp.bfloat16)

def right_block(image):
    nvecs = image.shape[-1]
    real_rows = image[0].reshape(-1, nvecs)
    imag_rows = image[1].reshape(-1, nvecs)
    first = jnp.concatenate([real_rows, imag_rows], 0)
    second = jnp.concatenate([imag_rows, -real_rows], 0)
    return jnp.concatenate([first, second], 1)

def reference(vectors, gauge_x, gauge_y):
    left_rows = vectors.reshape(-1, NV)
    image_x = colour_apply(gauge_x, jnp.roll(vectors, -1, 2))
    image_y = colour_apply(gauge_y, jnp.roll(vectors, -1, 3))
    right_cols = jnp.concatenate([right_block(image_x), right_block(image_y)], 1)
    partial_value = jnp.dot(left_rows.T, right_cols, preferred_element_type=jnp.float32)
    scaling = 1.0 / math.sqrt(3.0 * NX * NY * LZ)
    return (partial_value * scaling).reshape(NV, 2, 2, NV).transpose(1, 2, 0, 3)
```

```python
import functools
import math

import jax
import jax.numpy as jnp
from jax import lax
from jax.experimental import pallas as pl
from jax.experimental.pallas import tpu as pltpu
from jax.sharding import PartitionSpec as P

MESH = pl.DeviceIdType.MESH


def kernel(
    ngx, nyz, scaling,
    v_hbm, gx_hbm, gy_hbm, out_ref,
    v, hy, gauge, vt, acc, part, landed,
    load_sem, gauge_sem, halo_send, halo_recv, rs_send, rs_recv, ag_send, ag_recv,
):
    nx, ny, nz, nv = v_hbm.shape[2:]
    rows = 3 * nz
    ranks = ngx * nyz
    chunk = 2 * nv // ranks
    my_x = lax.axis_index("gx")
    my_y = lax.axis_index("yz")
    me = my_x * nyz + my_y

    def gauge_copy(d):
        return pltpu.make_async_copy((gx_hbm, gy_hbm)[d], gauge.at[d], gauge_sem.at[d])

    def row_copy(x):
        return pltpu.make_async_copy(v_hbm.at[:, :, x], v.at[:, :, x], load_sem.at[x])

    gauge_copy(0).start()
    for x in range(nx):
        row_copy(x).start()
    gauge_copy(1).start()

    def peer(k):
        kx, ky = k // nyz, k % nyz
        return lax.rem(my_x + kx, ngx), lax.rem(my_y + ky, nyz)

    barrier = pltpu.get_barrier_semaphore()
    for k in range(1, ranks):
        px, py = peer(k)
        pl.semaphore_signal(
            barrier, inc=1, device_id={"gx": px, "yz": py}, device_id_type=MESH
        )
    pl.semaphore_wait(barrier, ranks - 1)

    halo_x = pltpu.make_async_remote_copy(
        src_ref=v_hbm.at[:, :, 0], dst_ref=v.at[:, :, nx],
        send_sem=halo_send.at[0], recv_sem=halo_recv.at[0],
        device_id={"gx": lax.rem(my_x + ngx - 1, ngx)}, device_id_type=MESH,
    )
    halo_y = pltpu.make_async_remote_copy(
        src_ref=v_hbm.at[:, :, :, 0], dst_ref=hy,
        send_sem=halo_send.at[1], recv_sem=halo_recv.at[1],
        device_id={"yz": lax.rem(my_y + nyz - 1, nyz)}, device_id_type=MESH,
    )
    halo_x.start()
    halo_y.start()

    lanes = lax.broadcasted_iota(jnp.int32, (nz, 2 * rows), 1) % nz
    subs = lax.broadcasted_iota(jnp.int32, (nz, 2 * rows), 0)
    diagonal = jnp.where(lanes == subs, 1.0, 0.0).astype(jnp.bfloat16)

    def links(d, x):
        found = []
        for a in range(3):
            pieces = [gauge[d, r, a, b, x] for r in range(2) for b in range(3)]
            full = jnp.concatenate(pieces, axis=1)
            high = full.astype(jnp.bfloat16).astype(jnp.float32)
            found.append((high, full - high))
        return found

    def spread(row):
        wide = jnp.broadcast_to(row, (nz, 2 * rows)).astype(jnp.bfloat16)
        return wide * diagonal

    def image(found, y, source):
        real = source[0].reshape(rows, nv)
        imag = source[1].reshape(rows, nv)
        weights = jnp.concatenate(
            [jnp.concatenate([real, -imag], 0), jnp.concatenate([imag, real], 0)], 1
        )
        parts = [spread(found[a][p][y : y + 1]) for p in range(2) for a in range(3)]
        both = jnp.dot(
            jnp.concatenate(parts, 0), weights, preferred_element_type=jnp.float32
        )
        return (both[:rows] + both[rows:]).astype(jnp.bfloat16)

    def left(sites):
        return jnp.concatenate(
            [
                jnp.concatenate([v[r, :, x, y].reshape(rows, nv) for x, y in sites], 0)
                for r in range(2)
            ],
            1,
        )

    def finish(d):
        total = acc[...]
        part[d, :nv] = total[:nv, :nv] + total[nv:, nv:]
        part[d, nv:] = total[:nv, nv:] - total[nv:, :nv]

    def scatter(d, k):
        px, py = peer(k)
        owner = px * nyz + py
        return pltpu.make_async_remote_copy(
            src_ref=part.at[d, pl.ds(pl.multiple_of(owner * chunk, chunk), chunk)],
            dst_ref=landed.at[d, k],
            send_sem=rs_send.at[d, k], recv_sem=rs_recv.at[d, k],
            device_id={"gx": px, "yz": py}, device_id_type=MESH,
        )

    mine = pl.ds(pl.multiple_of(me * chunk, chunk), chunk)

    def gather(d, k):
        px, py = peer(k)
        return pltpu.make_async_remote_copy(
            src_ref=out_ref.at[d, mine],
            dst_ref=out_ref.at[d, mine],
            send_sem=ag_send.at[d, k], recv_sem=ag_recv.at[d, k],
            device_id={"gx": px, "yz": py}, device_id_type=MESH,
        )

    def reduce_and_gather(d):
        total = part[d, mine]
        for k in range(1, ranks):
            scatter(d, k).wait_recv()
            total = total + landed[d, k]
        out_ref[d, mine] = total * scaling
        for k in range(1, ranks):
            gather(d, k).start()

    acc[...] = jnp.zeros_like(acc)
    gauge_copy(0).wait()
    row_copy(0).wait()

    @pl.loop(0, nx)
    def _(x):
        @pl.when(x < nx - 1)
        def _():
            row_copy(x + 1).wait()

        @pl.when(x == nx - 1)
        def _():
            halo_x.wait_recv()

        turned = left([(x, y) for y in range(ny)]).T
        vt[x] = turned
        found = links(0, x)
        images = [image(found, y, v[:, :, x + 1, y]) for y in range(ny)]
        acc[...] += jnp.dot(
            turned, jnp.concatenate(images, 0), preferred_element_type=jnp.float32
        )

    finish(0)
    for k in range(1, ranks):
        scatter(0, k).start()

    acc[...] = jnp.zeros_like(acc)
    gauge_copy(1).wait()

    @pl.loop(0, nx)
    def _(x):
        found = links(1, x)
        images = [image(found, y, v[:, :, x, y + 1]) for y in range(ny - 1)]
        images.append(jnp.zeros((rows, 2 * nv), jnp.bfloat16))
        acc[...] += jnp.dot(
            vt[x], jnp.concatenate(images, 0), preferred_element_type=jnp.float32
        )

    reduce_and_gather(0)
    halo_y.wait_recv()
    images = [image(links(1, x), ny - 1, hy[:, :, x]) for x in range(nx)]
    acc[...] += jnp.dot(
        left([(x, ny - 1) for x in range(nx)]).T, jnp.concatenate(images, 0),
        preferred_element_type=jnp.float32,
    )
    finish(1)
    for k in range(1, ranks):
        scatter(1, k).start()
    reduce_and_gather(1)

    for d in range(2):
        for k in range(1, ranks):
            gather(d, k).wait_recv()
    halo_x.wait_send()
    halo_y.wait_send()
    for d in range(2):
        for k in range(1, ranks):
            scatter(d, k).wait_send()
            gather(d, k).wait_send()


def local(vectors, gauge_x, gauge_y):
    ngx, nyz = lax.axis_size("gx"), lax.axis_size("yz")
    _, _, nx, ny, nz, nv = vectors.shape
    ranks = ngx * nyz
    scaling = 1.0 / math.sqrt(3.0 * nx * ngx * ny * nyz * nz)
    sites = 3 * nx * ny * nz
    out = pl.pallas_call(
        functools.partial(kernel, ngx, nyz, scaling),
        out_shape=jax.ShapeDtypeStruct((2, 2 * nv, nv), jnp.float32),
        in_specs=[pl.BlockSpec(memory_space=pl.ANY)] * 3,
        out_specs=pl.BlockSpec(memory_space=pltpu.VMEM),
        scratch_shapes=[
            pltpu.VMEM((2, 3, nx + 1, ny, nz, nv), jnp.bfloat16),
            pltpu.VMEM((2, 3, nx, nz, nv), jnp.bfloat16),
            pltpu.VMEM((2,) + gauge_x.shape, jnp.float32),
            pltpu.VMEM((nx, 2 * nv, 3 * ny * nz), jnp.bfloat16),
            pltpu.VMEM((2 * nv, 2 * nv), jnp.float32),
            pltpu.VMEM((2, 2 * nv, nv), jnp.float32),
            pltpu.VMEM((2, ranks, 2 * nv // ranks, nv), jnp.float32),
            pltpu.SemaphoreType.DMA((nx,)),
            pltpu.SemaphoreType.DMA((2,)),
            pltpu.SemaphoreType.DMA((2,)),
            pltpu.SemaphoreType.DMA((2,)),
            pltpu.SemaphoreType.DMA((2, ranks)),
            pltpu.SemaphoreType.DMA((2, ranks)),
            pltpu.SemaphoreType.DMA((2, ranks)),
            pltpu.SemaphoreType.DMA((2, ranks)),
        ],
        compiler_params=pltpu.CompilerParams(
            collective_id=0, has_side_effects=True, vmem_limit_bytes=32 * 1024 * 1024
        ),
        cost_estimate=pl.CostEstimate(
            flops=24 * sites * nv * nv, bytes_accessed=4 * sites * nv, transcendentals=0
        ),
        name="elementals",
    )(vectors, gauge_x, gauge_y)
    return out.reshape(2, 2, nv, nv)


def solution(mesh):
    placed = (
        P(None, None, "gx", "yz", "ta", None),
        P(None, None, None, "gx", "yz", "ta"),
        P(None, None, None, "gx", "yz", "ta"),
    )
    return jax.shard_map(
        local, mesh=mesh, in_specs=placed, out_specs=P("ta", None, None, None), check_vma=False
    )
```

```python
import functools
import math

import jax
import jax.numpy as jnp
from jax import lax
from jax.experimental import pallas as pl
from jax.experimental.pallas import tpu as pltpu
from jax.sharding import PartitionSpec as P

MESH = pl.DeviceIdType.MESH


def kernel(
    ngx, nyz, scaling,
    v_hbm, gx_hbm, gy_hbm, out_ref,
    v, hy, gauge, vt, acc, part, swapped, landed,
    load_sem, gauge_sem, halo_send, halo_recv, swap_send, swap_recv,
    rs_send, rs_recv, ag_send, ag_recv, fw_send, fw_recv,
):
    nx, ny, nz, nv = v_hbm.shape[2:]
    rows = 3 * nz
    half_gx = ngx // 2
    chips = half_gx * nyz
    chunk = nv // chips
    my_x = lax.axis_index("gx")
    my_y = lax.axis_index("yz")
    core = lax.rem(my_x, 2)
    me = (my_x // 2) * nyz + my_y

    def gauge_copy(d):
        return pltpu.make_async_copy((gx_hbm, gy_hbm)[d], gauge.at[d], gauge_sem.at[d])

    def row_copy(x):
        return pltpu.make_async_copy(v_hbm.at[:, :, x], v.at[:, :, x], load_sem.at[x])

    gauge_copy(0).start()
    for x in range(nx):
        row_copy(x).start()
    gauge_copy(1).start()

    def peer(k):
        kx, ky = k // nyz, k % nyz
        return lax.rem(my_x + 2 * kx, ngx), lax.rem(my_y + ky, nyz)

    barrier = pltpu.get_barrier_semaphore()
    for kx in range(ngx):
        for ky in range(nyz):
            if (kx, ky) != (0, 0):
                pl.semaphore_signal(
                    barrier, inc=1,
                    device_id={
                        "gx": lax.rem(my_x + kx, ngx), "yz": lax.rem(my_y + ky, nyz)
                    },
                    device_id_type=MESH,
                )
    pl.semaphore_wait(barrier, ngx * nyz - 1)

    halo_x = pltpu.make_async_remote_copy(
        src_ref=v_hbm.at[:, :, 0], dst_ref=v.at[:, :, nx],
        send_sem=halo_send.at[0], recv_sem=halo_recv.at[0],
        device_id={"gx": lax.rem(my_x + ngx - 1, ngx)}, device_id_type=MESH,
    )
    halo_y = pltpu.make_async_remote_copy(
        src_ref=v_hbm.at[:, :, :, 0], dst_ref=hy,
        send_sem=halo_send.at[1], recv_sem=halo_recv.at[1],
        device_id={"yz": lax.rem(my_y + nyz - 1, nyz)}, device_id_type=MESH,
    )
    halo_x.start()
    halo_y.start()

    lanes = lax.broadcasted_iota(jnp.int32, (nz, 2 * rows), 1) % nz
    subs = lax.broadcasted_iota(jnp.int32, (nz, 2 * rows), 0)
    diagonal = jnp.where(lanes == subs, 1.0, 0.0).astype(jnp.bfloat16)

    def links(d, x):
        found = []
        for a in range(3):
            pieces = [gauge[d, r, a, b, x] for r in range(2) for b in range(3)]
            full = jnp.concatenate(pieces, axis=1)
            high = full.astype(jnp.bfloat16).astype(jnp.float32)
            found.append((high, full - high))
        return found

    def spread(row):
        wide = jnp.broadcast_to(row, (nz, 2 * rows)).astype(jnp.bfloat16)
        return wide * diagonal

    def image(found, y, source):
        real = source[0].reshape(rows, nv)
        imag = source[1].reshape(rows, nv)
        weights = jnp.concatenate(
            [jnp.concatenate([real, -imag], 0), jnp.concatenate([imag, real], 0)], 1
        )
        parts = [spread(found[a][p][y : y + 1]) for p in range(2) for a in range(3)]
        both = jnp.dot(
            jnp.concatenate(parts, 0), weights, preferred_element_type=jnp.float32
        )
        return (both[:rows] + both[rows:]).astype(jnp.bfloat16)

    def left(sites):
        return jnp.concatenate(
            [
                jnp.concatenate([v[r, :, x, y].reshape(rows, nv) for x, y in sites], 0)
                for r in range(2)
            ],
            1,
        )

    def finish(d):
        total = acc[...]
        part[d, :nv] = total[:nv, :nv] + total[nv:, nv:]
        part[d, nv:] = total[:nv, nv:] - total[nv:, :nv]

    sibling = {"gx": my_x + 1 - 2 * core}
    half = pl.ds(pl.multiple_of(core * nv, nv), nv)
    other_half = pl.ds(pl.multiple_of((1 - core) * nv, nv), nv)

    def chunk_of(owner):
        return pl.ds(pl.multiple_of(core * nv + owner * chunk, chunk), chunk)

    def swap(d):
        return pltpu.make_async_remote_copy(
            src_ref=part.at[d, other_half], dst_ref=swapped.at[d],
            send_sem=swap_send.at[d], recv_sem=swap_recv.at[d],
            device_id=sibling, device_id_type=MESH,
        )

    def scatter(d, k):
        px, py = peer(k)
        owner = (px // 2) * nyz + py
        return pltpu.make_async_remote_copy(
            src_ref=part.at[d, chunk_of(owner)], dst_ref=landed.at[d, k],
            send_sem=rs_send.at[d, k], recv_sem=rs_recv.at[d, k],
            device_id={"gx": px, "yz": py}, device_id_type=MESH,
        )

    def gather(d, k):
        px, py = peer(k)
        return pltpu.make_async_remote_copy(
            src_ref=out_ref.at[d, chunk_of(me)], dst_ref=out_ref.at[d, chunk_of(me)],
            send_sem=ag_send.at[d, k], recv_sem=ag_recv.at[d, k],
            device_id={"gx": px, "yz": py}, device_id_type=MESH,
        )

    def forward(d, k):
        fx = lax.rem(my_x // 2 + half_gx - k // nyz, half_gx)
        fy = lax.rem(my_y + nyz - k % nyz, nyz)
        rows_k = chunk_of(fx * nyz + fy)
        return pltpu.make_async_remote_copy(
            src_ref=out_ref.at[d, rows_k], dst_ref=out_ref.at[d, rows_k],
            send_sem=fw_send.at[d, k], recv_sem=fw_recv.at[d, k],
            device_id=sibling, device_id_type=MESH,
        )

    def start_scatter(d):
        swap(d).wait_recv()
        part[d, half] = part[d, half] + swapped[d]
        for k in range(1, chips):
            scatter(d, k).start()

    def reduce_and_gather(d):
        total = part[d, chunk_of(me)]
        for k in range(1, chips):
            scatter(d, k).wait_recv()
            total = total + landed[d, k]
        out_ref[d, chunk_of(me)] = total * scaling
        for k in range(1, chips):
            gather(d, k).start()
        forward(d, 0).start()

    def pass_on(d):
        for k in range(1, chips):
            gather(d, k).wait_recv()
            forward(d, k).start()

    acc[...] = jnp.zeros_like(acc)
    gauge_copy(0).wait()
    row_copy(0).wait()

    @pl.loop(0, nx)
    def _(x):
        @pl.when(x < nx - 1)
        def _():
            row_copy(x + 1).wait()

        @pl.when(x == nx - 1)
        def _():
            halo_x.wait_recv()

        turned = left([(x, y) for y in range(ny)]).T
        vt[x] = turned
        found = links(0, x)
        images = [image(found, y, v[:, :, x + 1, y]) for y in range(ny)]
        acc[...] += jnp.dot(
            turned, jnp.concatenate(images, 0), preferred_element_type=jnp.float32
        )

    finish(0)
    swap(0).start()

    acc[...] = jnp.zeros_like(acc)
    gauge_copy(1).wait()

    @pl.loop(0, nx)
    def _(x):
        @pl.when(x == 2)
        def _():
            start_scatter(0)

        found = links(1, x)
        images = [image(found, y, v[:, :, x, y + 1]) for y in range(ny - 1)]
        images.append(jnp.zeros((rows, 2 * nv), jnp.bfloat16))
        acc[...] += jnp.dot(
            vt[x], jnp.concatenate(images, 0), preferred_element_type=jnp.float32
        )

    reduce_and_gather(0)
    halo_y.wait_recv()
    images = [image(links(1, x), ny - 1, hy[:, :, x]) for x in range(nx)]
    acc[...] += jnp.dot(
        left([(x, ny - 1) for x in range(nx)]).T, jnp.concatenate(images, 0),
        preferred_element_type=jnp.float32,
    )
    finish(1)
    swap(1).start()
    pass_on(0)
    start_scatter(1)
    reduce_and_gather(1)
    pass_on(1)

    for d in range(2):
        for k in range(chips):
            forward(d, k).wait_recv()
    halo_x.wait_send()
    halo_y.wait_send()
    for d in range(2):
        swap(d).wait_send()
        for k in range(chips):
            forward(d, k).wait_send()
            if k > 0:
                scatter(d, k).wait_send()
                gather(d, k).wait_send()


def local(vectors, gauge_x, gauge_y):
    ngx, nyz = lax.axis_size("gx"), lax.axis_size("yz")
    _, _, nx, ny, nz, nv = vectors.shape
    chips = ngx // 2 * nyz
    scaling = 1.0 / math.sqrt(3.0 * nx * ngx * ny * nyz * nz)
    sites = 3 * nx * ny * nz
    out = pl.pallas_call(
        functools.partial(kernel, ngx, nyz, scaling),
        out_shape=jax.ShapeDtypeStruct((2, 2 * nv, nv), jnp.float32),
        in_specs=[pl.BlockSpec(memory_space=pl.ANY)] * 3,
        out_specs=pl.BlockSpec(memory_space=pltpu.VMEM),
        scratch_shapes=[
            pltpu.VMEM((2, 3, nx + 1, ny, nz, nv), jnp.bfloat16),
            pltpu.VMEM((2, 3, nx, nz, nv), jnp.bfloat16),
            pltpu.VMEM((2,) + gauge_x.shape, jnp.float32),
            pltpu.VMEM((nx, 2 * nv, 3 * ny * nz), jnp.bfloat16),
            pltpu.VMEM((2 * nv, 2 * nv), jnp.float32),
            pltpu.VMEM((2, 2 * nv, nv), jnp.float32),
            pltpu.VMEM((2, nv, nv), jnp.float32),
            pltpu.VMEM((2, chips, nv // chips, nv), jnp.float32),
            pltpu.SemaphoreType.DMA((nx,)),
            pltpu.SemaphoreType.DMA((2,)),
            pltpu.SemaphoreType.DMA((2,)),
            pltpu.SemaphoreType.DMA((2,)),
            pltpu.SemaphoreType.DMA((2,)),
            pltpu.SemaphoreType.DMA((2,)),
            pltpu.SemaphoreType.DMA((2, chips)),
            pltpu.SemaphoreType.DMA((2, chips)),
            pltpu.SemaphoreType.DMA((2, chips)),
            pltpu.SemaphoreType.DMA((2, chips)),
            pltpu.SemaphoreType.DMA((2, chips)),
            pltpu.SemaphoreType.DMA((2, chips)),
        ],
        compiler_params=pltpu.CompilerParams(
            collective_id=0, has_side_effects=True, vmem_limit_bytes=63 * 1024 * 1024
        ),
        cost_estimate=pl.CostEstimate(
            flops=24 * sites * nv * nv, bytes_accessed=4 * sites * nv, transcendentals=0
        ),
        name="elementals",
    )(vectors, gauge_x, gauge_y)
    return out.reshape(2, 2, nv, nv)


def solution(mesh):
    placed = (
        P(None, None, "gx", "yz", "ta", None),
        P(None, None, None, "gx", "yz", "ta"),
        P(None, None, None, "gx", "yz", "ta"),
    )
    return jax.shard_map(
        local, mesh=mesh, in_specs=placed, out_specs=P("ta", None, None, None), check_vma=False
    )
```

```python
import functools
import math

import jax
import jax.numpy as jnp
from jax import lax
from jax.experimental import pallas as pl
from jax.experimental.pallas import tpu as pltpu
from jax.sharding import PartitionSpec as P

MESH = pl.DeviceIdType.MESH
GROUP_X = 2
GROUP_Y = 4


def kernel(
    ngx, nyz,
    v_hbm, gx_hbm, gy_hbm, out_ref,
    v, hy, gauge, vt, acc, part, swapped, landed,
    load_sem, gauge_sem, halo_send, halo_recv, swap_send, swap_recv,
    rs_send, rs_recv, ag_send, ag_recv, fw_send, fw_recv,
):
    nx, ny, nz, nv = v_hbm.shape[2:]
    rows = 3 * nz
    half_gx = ngx // 2
    chips = half_gx * nyz
    chunk = nv // chips
    my_x = lax.axis_index("gx")
    my_y = lax.axis_index("yz")
    core = lax.rem(my_x, 2)
    me = (my_x // 2) * nyz + my_y

    def gauge_copy(d):
        return pltpu.make_async_copy((gx_hbm, gy_hbm)[d], gauge.at[d], gauge_sem.at[d])

    def row_copy(x):
        return pltpu.make_async_copy(v_hbm.at[:, :, x], v.at[:, :, x], load_sem.at[x])

    gauge_copy(0).start()
    for x in range(nx):
        row_copy(x).start()
    gauge_copy(1).start()

    def peer(k):
        kx, ky = k // nyz, k % nyz
        return lax.rem(my_x + 2 * kx, ngx), lax.rem(my_y + ky, nyz)

    barrier = pltpu.get_barrier_semaphore()
    for kx in range(ngx):
        for ky in range(nyz):
            if (kx, ky) != (0, 0):
                pl.semaphore_signal(
                    barrier, inc=1,
                    device_id={
                        "gx": lax.rem(my_x + kx, ngx), "yz": lax.rem(my_y + ky, nyz)
                    },
                    device_id_type=MESH,
                )

    halo_x = pltpu.make_async_remote_copy(
        src_ref=v_hbm.at[:, :, 0], dst_ref=v.at[:, :, nx],
        send_sem=halo_send.at[0], recv_sem=halo_recv.at[0],
        device_id={"gx": lax.rem(my_x + ngx - 1, ngx)}, device_id_type=MESH,
    )
    halo_y = pltpu.make_async_remote_copy(
        src_ref=v_hbm.at[:, :, :, 0], dst_ref=hy,
        send_sem=halo_send.at[1], recv_sem=halo_recv.at[1],
        device_id={"yz": lax.rem(my_y + nyz - 1, nyz)}, device_id_type=MESH,
    )
    lanes = lax.broadcasted_iota(jnp.int32, (nz, 2 * rows), 1) % nz
    subs = lax.broadcasted_iota(jnp.int32, (nz, 2 * rows), 0)
    diagonal = jnp.where(lanes == subs, 1.0, 0.0).astype(jnp.bfloat16)

    def links(d, x):
        found = []
        for a in range(3):
            pieces = [gauge[d, r, a, b, x] for r in range(2) for b in range(3)]
            full = jnp.concatenate(pieces, axis=1)
            high = full.astype(jnp.bfloat16).astype(jnp.float32)
            found.append((high, full - high))
        return found

    def spread(row):
        wide = jnp.broadcast_to(row, (nz, 2 * rows)).astype(jnp.bfloat16)
        return wide * diagonal

    def image(found, y, source):
        real = source[0].reshape(rows, nv)
        imag = source[1].reshape(rows, nv)
        weights = jnp.concatenate(
            [jnp.concatenate([real, -imag], 0), jnp.concatenate([imag, real], 0)], 1
        )
        parts = [spread(found[a][p][y : y + 1]) for p in range(2) for a in range(3)]
        both = jnp.dot(
            jnp.concatenate(parts, 0), weights, preferred_element_type=jnp.float32
        )
        return (both[:rows] + both[rows:]).astype(jnp.bfloat16)

    def left(sites):
        return jnp.concatenate(
            [
                jnp.concatenate([v[r, :, x, y].reshape(rows, nv) for x, y in sites], 0)
                for r in range(2)
            ],
            1,
        )

    def finish(d):
        total = acc[...]
        part[d, :nv] = total[:nv, :nv] + total[nv:, nv:]
        part[d, nv:] = total[:nv, nv:] - total[nv:, :nv]

    sibling = {"gx": my_x + 1 - 2 * core}
    half = pl.ds(pl.multiple_of(core * nv, nv), nv)
    other_half = pl.ds(pl.multiple_of((1 - core) * nv, nv), nv)

    def chunk_of(owner):
        return pl.ds(pl.multiple_of(core * nv + owner * chunk, chunk), chunk)

    def swap(d):
        return pltpu.make_async_remote_copy(
            src_ref=part.at[d, other_half], dst_ref=swapped.at[d],
            send_sem=swap_send.at[d], recv_sem=swap_recv.at[d],
            device_id=sibling, device_id_type=MESH,
        )

    def scatter(d, k):
        px, py = peer(k)
        owner = (px // 2) * nyz + py
        return pltpu.make_async_remote_copy(
            src_ref=part.at[d, chunk_of(owner)], dst_ref=landed.at[d, k],
            send_sem=rs_send.at[d, k], recv_sem=rs_recv.at[d, k],
            device_id={"gx": px, "yz": py}, device_id_type=MESH,
        )

    def gather(d, k):
        px, py = peer(k)
        return pltpu.make_async_remote_copy(
            src_ref=out_ref.at[d, chunk_of(me)], dst_ref=out_ref.at[d, chunk_of(me)],
            send_sem=ag_send.at[d, k], recv_sem=ag_recv.at[d, k],
            device_id={"gx": px, "yz": py}, device_id_type=MESH,
        )

    def forward(d, k):
        fx = lax.rem(my_x // 2 + half_gx - k // nyz, half_gx)
        fy = lax.rem(my_y + nyz - k % nyz, nyz)
        rows_k = chunk_of(fx * nyz + fy)
        return pltpu.make_async_remote_copy(
            src_ref=out_ref.at[d, rows_k], dst_ref=out_ref.at[d, rows_k],
            send_sem=fw_send.at[d, k], recv_sem=fw_recv.at[d, k],
            device_id=sibling, device_id_type=MESH,
        )

    def start_scatter(d):
        swap(d).wait_recv()
        part[d, half] = part[d, half] + swapped[d]
        for k in range(1, chips):
            scatter(d, k).start()

    def reduce_and_gather(d):
        total = part[d, chunk_of(me)]
        for k in range(1, chips):
            scatter(d, k).wait_recv()
            total = total + landed[d, k]
        out_ref[d, chunk_of(me)] = total
        for k in range(1, chips):
            gather(d, k).start()
        forward(d, 0).start()

    def pass_on(d):
        for k in range(1, chips):
            gather(d, k).wait_recv()
            forward(d, k).start()

    acc[...] = jnp.zeros_like(acc)
    gauge_copy(0).wait()
    row_copy(0).wait()

    def rows_x(first):
        for x in [first + i for i in range(GROUP_X)]:
            turned = left([(x, y) for y in range(ny)]).T
            vt[x] = turned
            found = links(0, x)
            images = [image(found, y, v[:, :, x + 1, y]) for y in range(ny)]
            acc[...] += jnp.dot(
                turned, jnp.concatenate(images, 0), preferred_element_type=jnp.float32
            )

    for x in range(1, GROUP_X + 1):
        row_copy(x).wait()
    rows_x(0)

    pl.semaphore_wait(barrier, ngx * nyz - 1)
    halo_x.start()
    halo_y.start()

    @pl.loop(1, nx // GROUP_X)
    def _(group):
        first = group * GROUP_X
        for i in range(1, GROUP_X):
            row_copy(first + i).wait()

        @pl.when(group < nx // GROUP_X - 1)
        def _():
            row_copy(first + GROUP_X).wait()

        @pl.when(group == nx // GROUP_X - 1)
        def _():
            halo_x.wait_recv()

        rows_x(first)

    finish(0)
    swap(0).start()

    acc[...] = jnp.zeros_like(acc)
    gauge_copy(1).wait()

    @pl.loop(0, nx // GROUP_Y)
    def _(group):
        @pl.when(group == 1)
        def _():
            start_scatter(0)

        for x in [group * GROUP_Y + i for i in range(GROUP_Y)]:
            found = links(1, x)
            images = [image(found, y, v[:, :, x, y + 1]) for y in range(ny - 1)]
            images.append(jnp.zeros((rows, 2 * nv), jnp.bfloat16))
            acc[...] += jnp.dot(
                vt[x], jnp.concatenate(images, 0), preferred_element_type=jnp.float32
            )

    reduce_and_gather(0)
    halo_y.wait_recv()
    images = [image(links(1, x), ny - 1, hy[:, :, x]) for x in range(nx)]
    acc[...] += jnp.dot(
        left([(x, ny - 1) for x in range(nx)]).T, jnp.concatenate(images, 0),
        preferred_element_type=jnp.float32,
    )
    finish(1)
    swap(1).start()
    pass_on(0)
    start_scatter(1)
    reduce_and_gather(1)
    pass_on(1)

    for d in range(2):
        for k in range(chips):
            forward(d, k).wait_recv()
    halo_x.wait_send()
    halo_y.wait_send()
    for d in range(2):
        swap(d).wait_send()
        for k in range(chips):
            forward(d, k).wait_send()
            if k > 0:
                scatter(d, k).wait_send()
                gather(d, k).wait_send()


def local(vectors, gauge_x, gauge_y):
    ngx, nyz = lax.axis_size("gx"), lax.axis_size("yz")
    _, _, nx, ny, nz, nv = vectors.shape
    chips = ngx // 2 * nyz
    scaling = 1.0 / math.sqrt(3.0 * nx * ngx * ny * nyz * nz)
    sites = 3 * nx * ny * nz
    out = pl.pallas_call(
        functools.partial(kernel, ngx, nyz),
        out_shape=jax.ShapeDtypeStruct((2, 2 * nv, nv), jnp.float32),
        in_specs=[pl.BlockSpec(memory_space=pl.ANY)] * 3,
        out_specs=pl.BlockSpec(memory_space=pltpu.VMEM),
        scratch_shapes=[
            pltpu.VMEM((2, 3, nx + 1, ny, nz, nv), jnp.bfloat16),
            pltpu.VMEM((2, 3, nx, nz, nv), jnp.bfloat16),
            pltpu.VMEM((2,) + gauge_x.shape, jnp.float32),
            pltpu.VMEM((nx, 2 * nv, 3 * ny * nz), jnp.bfloat16),
            pltpu.VMEM((2 * nv, 2 * nv), jnp.float32),
            pltpu.VMEM((2, 2 * nv, nv), jnp.float32),
            pltpu.VMEM((2, nv, nv), jnp.float32),
            pltpu.VMEM((2, chips, nv // chips, nv), jnp.float32),
            pltpu.SemaphoreType.DMA((nx,)),
            pltpu.SemaphoreType.DMA((2,)),
            pltpu.SemaphoreType.DMA((2,)),
            pltpu.SemaphoreType.DMA((2,)),
            pltpu.SemaphoreType.DMA((2,)),
            pltpu.SemaphoreType.DMA((2,)),
            pltpu.SemaphoreType.DMA((2, chips)),
            pltpu.SemaphoreType.DMA((2, chips)),
            pltpu.SemaphoreType.DMA((2, chips)),
            pltpu.SemaphoreType.DMA((2, chips)),
            pltpu.SemaphoreType.DMA((2, chips)),
            pltpu.SemaphoreType.DMA((2, chips)),
        ],
        compiler_params=pltpu.CompilerParams(
            collective_id=0, has_side_effects=True, vmem_limit_bytes=63 * 1024 * 1024
        ),
        cost_estimate=pl.CostEstimate(
            flops=24 * sites * nv * nv, bytes_accessed=4 * sites * nv, transcendentals=0
        ),
        name="elementals",
    )(vectors, gauge_x, gauge_y)
    return (out * scaling).reshape(2, 2, nv, nv)


def solution(mesh):
    placed = (
        P(None, None, "gx", "yz", "ta", None),
        P(None, None, None, "gx", "yz", "ta"),
        P(None, None, None, "gx", "yz", "ta"),
    )
    return jax.shard_map(
        local, mesh=mesh, in_specs=placed, out_specs=P("ta", None, None, None), check_vma=False
    )
```

```python
import functools
import math

import jax
import jax.numpy as jnp
from jax import lax
from jax.experimental import pallas as pl
from jax.experimental.pallas import tpu as pltpu
from jax.sharding import PartitionSpec as P

MESH = pl.DeviceIdType.MESH
GROUP_X = 1
GROUP_Y = 1


def kernel(
    ngx, nyz,
    v_hbm, gx_hbm, gy_hbm, out_ref,
    v, hy, gauge, vt, acc, part, swapped, landed,
    load_sem, gauge_sem, halo_send, halo_recv, swap_send, swap_recv,
    rs_send, rs_recv, ag_send, ag_recv, fw_send, fw_recv,
):
    nx, ny, nz, nv = v_hbm.shape[2:]
    rows = 3 * nz
    half_gx = ngx // 2
    chips = half_gx * nyz
    chunk = nv // chips
    my_x = lax.axis_index("gx")
    my_y = lax.axis_index("yz")
    core = lax.rem(my_x, 2)
    me = (my_x // 2) * nyz + my_y

    def gauge_copy(d):
        return pltpu.make_async_copy((gx_hbm, gy_hbm)[d], gauge.at[d], gauge_sem.at[d])

    def row_copy(x):
        return pltpu.make_async_copy(v_hbm.at[:, :, x], v.at[:, :, x], load_sem.at[x])

    gauge_copy(0).start()
    for x in range(nx):
        row_copy(x).start()
    gauge_copy(1).start()

    def peer(k):
        kx, ky = k // nyz, k % nyz
        return lax.rem(my_x + 2 * kx, ngx), lax.rem(my_y + ky, nyz)

    barrier = pltpu.get_barrier_semaphore()
    for kx in range(ngx):
        for ky in range(nyz):
            if (kx, ky) != (0, 0):
                pl.semaphore_signal(
                    barrier, inc=1,
                    device_id={
                        "gx": lax.rem(my_x + kx, ngx), "yz": lax.rem(my_y + ky, nyz)
                    },
                    device_id_type=MESH,
                )

    halo_x = pltpu.make_async_remote_copy(
        src_ref=v_hbm.at[:, :, 0], dst_ref=v.at[:, :, nx],
        send_sem=halo_send.at[0], recv_sem=halo_recv.at[0],
        device_id={"gx": lax.rem(my_x + ngx - 1, ngx)}, device_id_type=MESH,
    )
    halo_y = pltpu.make_async_remote_copy(
        src_ref=v_hbm.at[:, :, :, 0], dst_ref=hy,
        send_sem=halo_send.at[1], recv_sem=halo_recv.at[1],
        device_id={"yz": lax.rem(my_y + nyz - 1, nyz)}, device_id_type=MESH,
    )
    def links(d, x):
        return gauge[d, :, :, :, x].reshape(18 * ny, nz).T

    def image(columns, y, source):
        def link(r, a, b):
            at = ((r * 3 + a) * 3 + b) * ny + y
            return columns[:, at : at + 1]

        wide = source.astype(jnp.float32)
        real_parts, imag_parts = [], []
        for a in range(3):
            real, imag = None, None
            for b in range(3):
                lr, li = link(0, a, b), link(1, a, b)
                r = lr * wide[0, b] - li * wide[1, b]
                i = lr * wide[1, b] + li * wide[0, b]
                real = r if real is None else real + r
                imag = i if imag is None else imag + i
            real_parts.append(real.astype(jnp.bfloat16))
            imag_parts.append(imag.astype(jnp.bfloat16))
        return jnp.concatenate(
            [jnp.concatenate(real_parts, 0), jnp.concatenate(imag_parts, 0)], 1
        )

    def left(sites):
        return jnp.concatenate(
            [
                jnp.concatenate([v[r, :, x, y].reshape(rows, nv) for x, y in sites], 0)
                for r in range(2)
            ],
            1,
        )

    def finish(d):
        total = acc[...]
        part[d, :nv] = total[:nv, :nv] + total[nv:, nv:]
        part[d, nv:] = total[:nv, nv:] - total[nv:, :nv]

    sibling = {"gx": my_x + 1 - 2 * core}
    half = pl.ds(pl.multiple_of(core * nv, nv), nv)
    other_half = pl.ds(pl.multiple_of((1 - core) * nv, nv), nv)

    def chunk_of(owner):
        return pl.ds(pl.multiple_of(core * nv + owner * chunk, chunk), chunk)

    def swap(d):
        return pltpu.make_async_remote_copy(
            src_ref=part.at[d, other_half], dst_ref=swapped.at[d],
            send_sem=swap_send.at[d], recv_sem=swap_recv.at[d],
            device_id=sibling, device_id_type=MESH,
        )

    def scatter(d, k):
        px, py = peer(k)
        owner = (px // 2) * nyz + py
        return pltpu.make_async_remote_copy(
            src_ref=part.at[d, chunk_of(owner)], dst_ref=landed.at[d, k],
            send_sem=rs_send.at[d, k], recv_sem=rs_recv.at[d, k],
            device_id={"gx": px, "yz": py}, device_id_type=MESH,
        )

    def gather(d, k):
        px, py = peer(k)
        return pltpu.make_async_remote_copy(
            src_ref=out_ref.at[d, chunk_of(me)], dst_ref=out_ref.at[d, chunk_of(me)],
            send_sem=ag_send.at[d, k], recv_sem=ag_recv.at[d, k],
            device_id={"gx": px, "yz": py}, device_id_type=MESH,
        )

    def forward(d, k):
        fx = lax.rem(my_x // 2 + half_gx - k // nyz, half_gx)
        fy = lax.rem(my_y + nyz - k % nyz, nyz)
        rows_k = chunk_of(fx * nyz + fy)
        return pltpu.make_async_remote_copy(
            src_ref=out_ref.at[d, rows_k], dst_ref=out_ref.at[d, rows_k],
            send_sem=fw_send.at[d, k], recv_sem=fw_recv.at[d, k],
            device_id=sibling, device_id_type=MESH,
        )

    def start_scatter(d):
        swap(d).wait_recv()
        part[d, half] = part[d, half] + swapped[d]
        for k in range(1, chips):
            scatter(d, k).start()

    def reduce_and_gather(d):
        total = part[d, chunk_of(me)]
        for k in range(1, chips):
            scatter(d, k).wait_recv()
            total = total + landed[d, k]
        out_ref[d, chunk_of(me)] = total
        for k in range(1, chips):
            gather(d, k).start()
        forward(d, 0).start()

    def pass_on(d):
        for k in range(1, chips):
            gather(d, k).wait_recv()
            forward(d, k).start()

    acc[...] = jnp.zeros_like(acc)
    gauge_copy(0).wait()
    row_copy(0).wait()

    def rows_x(first):
        for x in [first + i for i in range(GROUP_X)]:
            turned = left([(x, y) for y in range(ny)]).T
            vt[x] = turned
            found = links(0, x)
            images = [image(found, y, v[:, :, x + 1, y]) for y in range(ny)]
            acc[...] += jnp.dot(
                turned, jnp.concatenate(images, 0), preferred_element_type=jnp.float32
            )

    for x in range(1, GROUP_X + 1):
        row_copy(x).wait()
    rows_x(0)

    pl.semaphore_wait(barrier, ngx * nyz - 1)
    halo_x.start()
    halo_y.start()

    @pl.loop(1, nx // GROUP_X)
    def _(group):
        first = group * GROUP_X
        for i in range(1, GROUP_X):
            row_copy(first + i).wait()

        @pl.when(group < nx // GROUP_X - 1)
        def _():
            row_copy(first + GROUP_X).wait()

        @pl.when(group == nx // GROUP_X - 1)
        def _():
            halo_x.wait_recv()

        rows_x(first)

    finish(0)
    swap(0).start()

    acc[...] = jnp.zeros_like(acc)
    gauge_copy(1).wait()

    @pl.loop(0, nx // GROUP_Y)
    def _(group):
        @pl.when(group == 2 // GROUP_Y)
        def _():
            start_scatter(0)

        for x in [group * GROUP_Y + i for i in range(GROUP_Y)]:
            found = links(1, x)
            images = [image(found, y, v[:, :, x, y + 1]) for y in range(ny - 1)]
            images.append(jnp.zeros((rows, 2 * nv), jnp.bfloat16))
            acc[...] += jnp.dot(
                vt[x], jnp.concatenate(images, 0), preferred_element_type=jnp.float32
            )

    reduce_and_gather(0)
    halo_y.wait_recv()
    images = [image(links(1, x), ny - 1, hy[:, :, x]) for x in range(nx)]
    acc[...] += jnp.dot(
        left([(x, ny - 1) for x in range(nx)]).T, jnp.concatenate(images, 0),
        preferred_element_type=jnp.float32,
    )
    finish(1)
    swap(1).start()
    pass_on(0)
    start_scatter(1)
    reduce_and_gather(1)
    pass_on(1)

    for d in range(2):
        for k in range(chips):
            forward(d, k).wait_recv()
    halo_x.wait_send()
    halo_y.wait_send()
    for d in range(2):
        swap(d).wait_send()
        for k in range(chips):
            forward(d, k).wait_send()
            if k > 0:
                scatter(d, k).wait_send()
                gather(d, k).wait_send()


def local(vectors, gauge_x, gauge_y):
    ngx, nyz = lax.axis_size("gx"), lax.axis_size("yz")
    _, _, nx, ny, nz, nv = vectors.shape
    chips = ngx // 2 * nyz
    scaling = 1.0 / math.sqrt(3.0 * nx * ngx * ny * nyz * nz)
    sites = 3 * nx * ny * nz
    out = pl.pallas_call(
        functools.partial(kernel, ngx, nyz),
        out_shape=jax.ShapeDtypeStruct((2, 2 * nv, nv), jnp.float32),
        in_specs=[pl.BlockSpec(memory_space=pl.ANY)] * 3,
        out_specs=pl.BlockSpec(memory_space=pltpu.VMEM),
        scratch_shapes=[
            pltpu.VMEM((2, 3, nx + 1, ny, nz, nv), jnp.bfloat16),
            pltpu.VMEM((2, 3, nx, nz, nv), jnp.bfloat16),
            pltpu.VMEM((2,) + gauge_x.shape, jnp.float32),
            pltpu.VMEM((nx, 2 * nv, 3 * ny * nz), jnp.bfloat16),
            pltpu.VMEM((2 * nv, 2 * nv), jnp.float32),
            pltpu.VMEM((2, 2 * nv, nv), jnp.float32),
            pltpu.VMEM((2, nv, nv), jnp.float32),
            pltpu.VMEM((2, chips, nv // chips, nv), jnp.float32),
            pltpu.SemaphoreType.DMA((nx,)),
            pltpu.SemaphoreType.DMA((2,)),
            pltpu.SemaphoreType.DMA((2,)),
            pltpu.SemaphoreType.DMA((2,)),
            pltpu.SemaphoreType.DMA((2,)),
            pltpu.SemaphoreType.DMA((2,)),
            pltpu.SemaphoreType.DMA((2, chips)),
            pltpu.SemaphoreType.DMA((2, chips)),
            pltpu.SemaphoreType.DMA((2, chips)),
            pltpu.SemaphoreType.DMA((2, chips)),
            pltpu.SemaphoreType.DMA((2, chips)),
            pltpu.SemaphoreType.DMA((2, chips)),
        ],
        compiler_params=pltpu.CompilerParams(
            collective_id=0, has_side_effects=True, vmem_limit_bytes=63 * 1024 * 1024
        ),
        cost_estimate=pl.CostEstimate(
            flops=24 * sites * nv * nv, bytes_accessed=4 * sites * nv, transcendentals=0
        ),
        name="elementals",
    )(vectors, gauge_x, gauge_y)
    return (out * scaling).reshape(2, 2, nv, nv)


def solution(mesh):
    placed = (
        P(None, None, "gx", "yz", "ta", None),
        P(None, None, None, "gx", "yz", "ta"),
        P(None, None, None, "gx", "yz", "ta"),
    )
    return jax.shard_map(
        local, mesh=mesh, in_specs=placed, out_specs=P("ta", None, None, None), check_vma=False
    )
```

```python
import functools
import math

import jax
import jax.numpy as jnp
from jax import lax
from jax.experimental import pallas as pl
from jax.experimental.pallas import tpu as pltpu
from jax.sharding import PartitionSpec as P

MESH = pl.DeviceIdType.MESH
GROUP_X = 1
GROUP_Y = 1


def kernel(
    ngx, nyz,
    v_hbm, gx_hbm, gy_hbm, out_ref,
    v, hy, gauge, vt, acc, part, swapped, landed,
    load_sem, gauge_sem, halo_send, halo_recv, swap_send, swap_recv,
    rs_send, rs_recv, ag_send, ag_recv, fw_send, fw_recv,
):
    nx, ny, nz, nv = v_hbm.shape[2:]
    rows = 3 * nz
    half_gx = ngx // 2
    chips = half_gx * nyz
    chunk = nv // chips
    my_x = lax.axis_index("gx")
    my_y = lax.axis_index("yz")
    core = lax.rem(my_x, 2)
    me = (my_x // 2) * nyz + my_y

    def gauge_copy(d):
        return pltpu.make_async_copy((gx_hbm, gy_hbm)[d], gauge.at[d], gauge_sem.at[d])

    def row_copy(x):
        return pltpu.make_async_copy(v_hbm.at[:, :, x], v.at[:, :, x], load_sem.at[x])

    gauge_copy(0).start()
    for x in range(nx):
        row_copy(x).start()
    gauge_copy(1).start()

    def peer(k):
        kx, ky = k // nyz, k % nyz
        return lax.rem(my_x + 2 * kx, ngx), lax.rem(my_y + ky, nyz)

    barrier = pltpu.get_barrier_semaphore()
    for kx in range(ngx):
        for ky in range(nyz):
            if (kx, ky) != (0, 0):
                pl.semaphore_signal(
                    barrier, inc=1,
                    device_id={
                        "gx": lax.rem(my_x + kx, ngx), "yz": lax.rem(my_y + ky, nyz)
                    },
                    device_id_type=MESH,
                )

    halo_x = pltpu.make_async_remote_copy(
        src_ref=v_hbm.at[:, :, 0], dst_ref=v.at[:, :, nx],
        send_sem=halo_send.at[0], recv_sem=halo_recv.at[0],
        device_id={"gx": lax.rem(my_x + ngx - 1, ngx)}, device_id_type=MESH,
    )
    halo_y = pltpu.make_async_remote_copy(
        src_ref=v_hbm.at[:, :, :, 0], dst_ref=hy,
        send_sem=halo_send.at[1], recv_sem=halo_recv.at[1],
        device_id={"yz": lax.rem(my_y + nyz - 1, nyz)}, device_id_type=MESH,
    )
    lanes = lax.broadcasted_iota(jnp.int32, (nz, 2 * rows), 1) % nz
    subs = lax.broadcasted_iota(jnp.int32, (nz, 2 * rows), 0)
    diagonal = jnp.where(lanes == subs, 1.0, 0.0).astype(jnp.bfloat16)

    def link_rows(d, x):
        found = []
        for a in range(3):
            pieces = [gauge[d, r, a, b, x] for r in range(2) for b in range(3)]
            full = jnp.concatenate(pieces, axis=1)
            high = full.astype(jnp.bfloat16).astype(jnp.float32)
            found.append((high, full - high))
        return found

    def spread(row):
        wide = jnp.broadcast_to(row, (nz, 2 * rows)).astype(jnp.bfloat16)
        return wide * diagonal

    def image_by_matmul(found, y, source):
        real = source[0].reshape(rows, nv)
        imag = source[1].reshape(rows, nv)
        weights = jnp.concatenate(
            [jnp.concatenate([real, -imag], 0), jnp.concatenate([imag, real], 0)], 1
        )
        parts = [spread(found[a][p][y : y + 1]) for p in range(2) for a in range(3)]
        both = jnp.dot(
            jnp.concatenate(parts, 0), weights, preferred_element_type=jnp.float32
        )
        return (both[:rows] + both[rows:]).astype(jnp.bfloat16)

    def links(d, x):
        return gauge[d, :, :, :, x].reshape(18 * ny, nz).T

    def image_by_products(columns, y, source):
        def link(r, a, b):
            at = ((r * 3 + a) * 3 + b) * ny + y
            return columns[:, at : at + 1]

        wide = source.astype(jnp.float32)
        real_parts, imag_parts = [], []
        for a in range(3):
            real, imag = None, None
            for b in range(3):
                lr, li = link(0, a, b), link(1, a, b)
                r = lr * wide[0, b] - li * wide[1, b]
                i = lr * wide[1, b] + li * wide[0, b]
                real = r if real is None else real + r
                imag = i if imag is None else imag + i
            real_parts.append(real.astype(jnp.bfloat16))
            imag_parts.append(imag.astype(jnp.bfloat16))
        return jnp.concatenate(
            [jnp.concatenate(real_parts, 0), jnp.concatenate(imag_parts, 0)], 1
        )

    def row_images(d, x, count, source_of):
        found, columns = link_rows(d, x), links(d, x)
        images = []
        for y in range(count):
            if y % 2 == 0:
                images.append(image_by_matmul(found, y, source_of(y)))
            else:
                images.append(image_by_products(columns, y, source_of(y)))
        return images

    def left(sites):
        return jnp.concatenate(
            [
                jnp.concatenate([v[r, :, x, y].reshape(rows, nv) for x, y in sites], 0)
                for r in range(2)
            ],
            1,
        )

    def finish(d):
        total = acc[...]
        part[d, :nv] = total[:nv, :nv] + total[nv:, nv:]
        part[d, nv:] = total[:nv, nv:] - total[nv:, :nv]

    sibling = {"gx": my_x + 1 - 2 * core}
    half = pl.ds(pl.multiple_of(core * nv, nv), nv)
    other_half = pl.ds(pl.multiple_of((1 - core) * nv, nv), nv)

    def chunk_of(owner):
        return pl.ds(pl.multiple_of(core * nv + owner * chunk, chunk), chunk)

    def swap(d):
        return pltpu.make_async_remote_copy(
            src_ref=part.at[d, other_half], dst_ref=swapped.at[d],
            send_sem=swap_send.at[d], recv_sem=swap_recv.at[d],
            device_id=sibling, device_id_type=MESH,
        )

    def scatter(d, k):
        px, py = peer(k)
        owner = (px // 2) * nyz + py
        return pltpu.make_async_remote_copy(
            src_ref=part.at[d, chunk_of(owner)], dst_ref=landed.at[d, k],
            send_sem=rs_send.at[d, k], recv_sem=rs_recv.at[d, k],
            device_id={"gx": px, "yz": py}, device_id_type=MESH,
        )

    def gather(d, k):
        px, py = peer(k)
        return pltpu.make_async_remote_copy(
            src_ref=out_ref.at[d, chunk_of(me)], dst_ref=out_ref.at[d, chunk_of(me)],
            send_sem=ag_send.at[d, k], recv_sem=ag_recv.at[d, k],
            device_id={"gx": px, "yz": py}, device_id_type=MESH,
        )

    def forward(d, k):
        fx = lax.rem(my_x // 2 + half_gx - k // nyz, half_gx)
        fy = lax.rem(my_y + nyz - k % nyz, nyz)
        rows_k = chunk_of(fx * nyz + fy)
        return pltpu.make_async_remote_copy(
            src_ref=out_ref.at[d, rows_k], dst_ref=out_ref.at[d, rows_k],
            send_sem=fw_send.at[d, k], recv_sem=fw_recv.at[d, k],
            device_id=sibling, device_id_type=MESH,
        )

    def start_scatter(d):
        swap(d).wait_recv()
        part[d, half] = part[d, half] + swapped[d]
        for k in range(1, chips):
            scatter(d, k).start()

    def reduce_and_gather(d):
        total = part[d, chunk_of(me)]
        for k in range(1, chips):
            scatter(d, k).wait_recv()
            total = total + landed[d, k]
        out_ref[d, chunk_of(me)] = total
        for k in range(1, chips):
            gather(d, k).start()
        forward(d, 0).start()

    def pass_on(d):
        for k in range(1, chips):
            gather(d, k).wait_recv()
            forward(d, k).start()

    acc[...] = jnp.zeros_like(acc)
    gauge_copy(0).wait()
    row_copy(0).wait()

    def rows_x(first):
        for x in [first + i for i in range(GROUP_X)]:
            turned = left([(x, y) for y in range(ny)]).T
            vt[x] = turned
            images = row_images(0, x, ny, lambda y: v[:, :, x + 1, y])
            acc[...] += jnp.dot(
                turned, jnp.concatenate(images, 0), preferred_element_type=jnp.float32
            )

    for x in range(1, GROUP_X + 1):
        row_copy(x).wait()
    rows_x(0)

    pl.semaphore_wait(barrier, ngx * nyz - 1)
    halo_x.start()
    halo_y.start()

    @pl.loop(1, nx // GROUP_X)
    def _(group):
        first = group * GROUP_X
        for i in range(1, GROUP_X):
            row_copy(first + i).wait()

        @pl.when(group < nx // GROUP_X - 1)
        def _():
            row_copy(first + GROUP_X).wait()

        @pl.when(group == nx // GROUP_X - 1)
        def _():
            halo_x.wait_recv()

        rows_x(first)

    finish(0)
    swap(0).start()

    acc[...] = jnp.zeros_like(acc)
    gauge_copy(1).wait()

    @pl.loop(0, nx // GROUP_Y)
    def _(group):
        @pl.when(group == 2 // GROUP_Y)
        def _():
            start_scatter(0)

        for x in [group * GROUP_Y + i for i in range(GROUP_Y)]:
            images = row_images(1, x, ny - 1, lambda y: v[:, :, x, y + 1])
            images.append(jnp.zeros((rows, 2 * nv), jnp.bfloat16))
            acc[...] += jnp.dot(
                vt[x], jnp.concatenate(images, 0), preferred_element_type=jnp.float32
            )

    reduce_and_gather(0)
    halo_y.wait_recv()
    images = []
    for x in range(nx):
        if x % 2 == 0:
            images.append(image_by_matmul(link_rows(1, x), ny - 1, hy[:, :, x]))
        else:
            images.append(image_by_products(links(1, x), ny - 1, hy[:, :, x]))
    acc[...] += jnp.dot(
        left([(x, ny - 1) for x in range(nx)]).T, jnp.concatenate(images, 0),
        preferred_element_type=jnp.float32,
    )
    finish(1)
    swap(1).start()
    pass_on(0)
    start_scatter(1)
    reduce_and_gather(1)
    pass_on(1)

    for d in range(2):
        for k in range(chips):
            forward(d, k).wait_recv()
    halo_x.wait_send()
    halo_y.wait_send()
    for d in range(2):
        swap(d).wait_send()
        for k in range(chips):
            forward(d, k).wait_send()
            if k > 0:
                scatter(d, k).wait_send()
                gather(d, k).wait_send()


def local(vectors, gauge_x, gauge_y):
    ngx, nyz = lax.axis_size("gx"), lax.axis_size("yz")
    _, _, nx, ny, nz, nv = vectors.shape
    chips = ngx // 2 * nyz
    scaling = 1.0 / math.sqrt(3.0 * nx * ngx * ny * nyz * nz)
    sites = 3 * nx * ny * nz
    out = pl.pallas_call(
        functools.partial(kernel, ngx, nyz),
        out_shape=jax.ShapeDtypeStruct((2, 2 * nv, nv), jnp.float32),
        in_specs=[pl.BlockSpec(memory_space=pl.ANY)] * 3,
        out_specs=pl.BlockSpec(memory_space=pltpu.VMEM),
        scratch_shapes=[
            pltpu.VMEM((2, 3, nx + 1, ny, nz, nv), jnp.bfloat16),
            pltpu.VMEM((2, 3, nx, nz, nv), jnp.bfloat16),
            pltpu.VMEM((2,) + gauge_x.shape, jnp.float32),
            pltpu.VMEM((nx, 2 * nv, 3 * ny * nz), jnp.bfloat16),
            pltpu.VMEM((2 * nv, 2 * nv), jnp.float32),
            pltpu.VMEM((2, 2 * nv, nv), jnp.float32),
            pltpu.VMEM((2, nv, nv), jnp.float32),
            pltpu.VMEM((2, chips, nv // chips, nv), jnp.float32),
            pltpu.SemaphoreType.DMA((nx,)),
            pltpu.SemaphoreType.DMA((2,)),
            pltpu.SemaphoreType.DMA((2,)),
            pltpu.SemaphoreType.DMA((2,)),
            pltpu.SemaphoreType.DMA((2,)),
            pltpu.SemaphoreType.DMA((2,)),
            pltpu.SemaphoreType.DMA((2, chips)),
            pltpu.SemaphoreType.DMA((2, chips)),
            pltpu.SemaphoreType.DMA((2, chips)),
            pltpu.SemaphoreType.DMA((2, chips)),
            pltpu.SemaphoreType.DMA((2, chips)),
            pltpu.SemaphoreType.DMA((2, chips)),
        ],
        compiler_params=pltpu.CompilerParams(
            collective_id=0, has_side_effects=True, vmem_limit_bytes=63 * 1024 * 1024
        ),
        cost_estimate=pl.CostEstimate(
            flops=24 * sites * nv * nv, bytes_accessed=4 * sites * nv, transcendentals=0
        ),
        name="elementals",
    )(vectors, gauge_x, gauge_y)
    return (out * scaling).reshape(2, 2, nv, nv)


def solution(mesh):
    placed = (
        P(None, None, "gx", "yz", "ta", None),
        P(None, None, None, "gx", "yz", "ta"),
        P(None, None, None, "gx", "yz", "ta"),
    )
    return jax.shard_map(
        local, mesh=mesh, in_specs=placed, out_specs=P("ta", None, None, None), check_vma=False
    )
```

```python
import functools
import math

import jax
import jax.numpy as jnp
from jax import lax
from jax.experimental import pallas as pl
from jax.experimental.pallas import tpu as pltpu
from jax.sharding import PartitionSpec as P

MESH = pl.DeviceIdType.MESH
GROUP_X = 2
GROUP_Y = 4


def kernel(
    ngx, nyz, scaling,
    v_hbm, gx_hbm, gy_hbm, out_ref,
    v, hy, gauge, vt, acc, part, swapped, landed,
    load_sem, gauge_sem, halo_send, halo_recv, swap_send, swap_recv,
    rs_send, rs_recv, ag_send, ag_recv, fw_send, fw_recv,
):
    nx, ny, nz, nv = v_hbm.shape[2:]
    rows = 3 * nz
    half_gx = ngx // 2
    chips = half_gx * nyz
    chunk = nv // chips
    my_x = lax.axis_index("gx")
    my_y = lax.axis_index("yz")
    core = lax.rem(my_x, 2)
    me = (my_x // 2) * nyz + my_y

    def gauge_copy(d):
        return pltpu.make_async_copy((gx_hbm, gy_hbm)[d], gauge.at[d], gauge_sem.at[d])

    def row_copy(x):
        return pltpu.make_async_copy(v_hbm.at[:, :, x], v.at[:, :, x], load_sem.at[x])

    gauge_copy(0).start()
    for x in range(nx):
        row_copy(x).start()
    gauge_copy(1).start()

    def peer(k):
        kx, ky = k // nyz, k % nyz
        return lax.rem(my_x + 2 * kx, ngx), lax.rem(my_y + ky, nyz)

    barrier = pltpu.get_barrier_semaphore()
    for kx in range(ngx):
        for ky in range(nyz):
            if (kx, ky) != (0, 0):
                pl.semaphore_signal(
                    barrier, inc=1,
                    device_id={
                        "gx": lax.rem(my_x + kx, ngx), "yz": lax.rem(my_y + ky, nyz)
                    },
                    device_id_type=MESH,
                )

    pl.semaphore_wait(barrier, ngx * nyz - 1)
    halo_x = pltpu.make_async_remote_copy(
        src_ref=v_hbm.at[:, :, 0], dst_ref=v.at[:, :, nx],
        send_sem=halo_send.at[0], recv_sem=halo_recv.at[0],
        device_id={"gx": lax.rem(my_x + ngx - 1, ngx)}, device_id_type=MESH,
    )
    halo_y = pltpu.make_async_remote_copy(
        src_ref=v_hbm.at[:, :, :, 0], dst_ref=hy,
        send_sem=halo_send.at[1], recv_sem=halo_recv.at[1],
        device_id={"yz": lax.rem(my_y + nyz - 1, nyz)}, device_id_type=MESH,
    )
    halo_x.start()
    halo_y.start()

    lanes = lax.broadcasted_iota(jnp.int32, (nz, 2 * rows), 1) % nz
    subs = lax.broadcasted_iota(jnp.int32, (nz, 2 * rows), 0)
    diagonal = jnp.where(lanes == subs, 1.0, 0.0).astype(jnp.bfloat16)

    def links(d, x):
        found = []
        for a in range(3):
            pieces = [gauge[d, r, a, b, x] for r in range(2) for b in range(3)]
            full = jnp.concatenate(pieces, axis=1)
            high = full.astype(jnp.bfloat16).astype(jnp.float32)
            found.append((high, full - high))
        return found

    def spread(row):
        wide = jnp.broadcast_to(row, (nz, 2 * rows)).astype(jnp.bfloat16)
        return wide * diagonal

    def image(found, y, source):
        real = source[0].reshape(rows, nv)
        imag = source[1].reshape(rows, nv)
        weights = jnp.concatenate(
            [jnp.concatenate([real, -imag], 0), jnp.concatenate([imag, real], 0)], 1
        )
        parts = [spread(found[a][p][y : y + 1]) for p in range(2) for a in range(3)]
        both = jnp.dot(
            jnp.concatenate(parts, 0), weights, preferred_element_type=jnp.float32
        )
        return (both[:rows] + both[rows:]).astype(jnp.bfloat16)

    def left(sites):
        return jnp.concatenate(
            [
                jnp.concatenate([v[r, :, x, y].reshape(rows, nv) for x, y in sites], 0)
                for r in range(2)
            ],
            1,
        )

    def finish(d):
        total = acc[...]
        part[d, :nv] = total[:nv, :nv] + total[nv:, nv:]
        part[d, nv:] = total[:nv, nv:] - total[nv:, :nv]

    sibling = {"gx": my_x + 1 - 2 * core}
    half = pl.ds(pl.multiple_of(core * nv, nv), nv)
    other_half = pl.ds(pl.multiple_of((1 - core) * nv, nv), nv)

    def chunk_of(owner):
        return pl.ds(pl.multiple_of(core * nv + owner * chunk, chunk), chunk)

    def swap(d):
        return pltpu.make_async_remote_copy(
            src_ref=part.at[d, other_half], dst_ref=swapped.at[d],
            send_sem=swap_send.at[d], recv_sem=swap_recv.at[d],
            device_id=sibling, device_id_type=MESH,
        )

    def scatter(d, k):
        px, py = peer(k)
        owner = (px // 2) * nyz + py
        return pltpu.make_async_remote_copy(
            src_ref=part.at[d, chunk_of(owner)], dst_ref=landed.at[d, k],
            send_sem=rs_send.at[d, k], recv_sem=rs_recv.at[d, k],
            device_id={"gx": px, "yz": py}, device_id_type=MESH,
        )

    def gather(d, k):
        px, py = peer(k)
        return pltpu.make_async_remote_copy(
            src_ref=out_ref.at[d, chunk_of(me)], dst_ref=out_ref.at[d, chunk_of(me)],
            send_sem=ag_send.at[d, k], recv_sem=ag_recv.at[d, k],
            device_id={"gx": px, "yz": py}, device_id_type=MESH,
        )

    def forward(d, k):
        fx = lax.rem(my_x // 2 + half_gx - k // nyz, half_gx)
        fy = lax.rem(my_y + nyz - k % nyz, nyz)
        rows_k = chunk_of(fx * nyz + fy)
        return pltpu.make_async_remote_copy(
            src_ref=out_ref.at[d, rows_k], dst_ref=out_ref.at[d, rows_k],
            send_sem=fw_send.at[d, k], recv_sem=fw_recv.at[d, k],
            device_id=sibling, device_id_type=MESH,
        )

    def start_scatter(d):
        swap(d).wait_recv()
        part[d, half] = part[d, half] + swapped[d]
        for k in range(1, chips):
            scatter(d, k).start()

    def reduce_and_gather(d):
        total = part[d, chunk_of(me)]
        for k in range(1, chips):
            scatter(d, k).wait_recv()
            total = total + landed[d, k]
        out_ref[d, chunk_of(me)] = total * scaling
        for k in range(1, chips):
            gather(d, k).start()
        forward(d, 0).start()

    def pass_on(d):
        for k in range(1, chips):
            gather(d, k).wait_recv()
            forward(d, k).start()

    acc[...] = jnp.zeros_like(acc)
    gauge_copy(0).wait()
    row_copy(0).wait()

    def rows_x(first):
        for x in [first + i for i in range(GROUP_X)]:
            turned = left([(x, y) for y in range(ny)]).T
            vt[x] = turned
            found = links(0, x)
            images = [image(found, y, v[:, :, x + 1, y]) for y in range(ny)]
            acc[...] += jnp.dot(
                turned, jnp.concatenate(images, 0), preferred_element_type=jnp.float32
            )

    for x in range(1, GROUP_X + 1):
        row_copy(x).wait()
    rows_x(0)


    @pl.loop(1, nx // GROUP_X)
    def _(group):
        first = group * GROUP_X
        for i in range(1, GROUP_X):
            row_copy(first + i).wait()

        @pl.when(group < nx // GROUP_X - 1)
        def _():
            row_copy(first + GROUP_X).wait()

        @pl.when(group == nx // GROUP_X - 1)
        def _():
            halo_x.wait_recv()

        rows_x(first)

    finish(0)
    swap(0).start()

    acc[...] = jnp.zeros_like(acc)
    gauge_copy(1).wait()

    @pl.loop(0, nx // GROUP_Y)
    def _(group):
        @pl.when(group == 1)
        def _():
            start_scatter(0)

        for x in [group * GROUP_Y + i for i in range(GROUP_Y)]:
            found = links(1, x)
            images = [image(found, y, v[:, :, x, y + 1]) for y in range(ny - 1)]
            images.append(jnp.zeros((rows, 2 * nv), jnp.bfloat16))
            acc[...] += jnp.dot(
                vt[x], jnp.concatenate(images, 0), preferred_element_type=jnp.float32
            )

    reduce_and_gather(0)
    halo_y.wait_recv()
    images = [image(links(1, x), ny - 1, hy[:, :, x]) for x in range(nx)]
    acc[...] += jnp.dot(
        left([(x, ny - 1) for x in range(nx)]).T, jnp.concatenate(images, 0),
        preferred_element_type=jnp.float32,
    )
    finish(1)
    swap(1).start()
    pass_on(0)
    start_scatter(1)
    reduce_and_gather(1)
    pass_on(1)

    for d in range(2):
        for k in range(chips):
            forward(d, k).wait_recv()
    halo_x.wait_send()
    halo_y.wait_send()
    for d in range(2):
        swap(d).wait_send()
        for k in range(chips):
            forward(d, k).wait_send()
            if k > 0:
                scatter(d, k).wait_send()
                gather(d, k).wait_send()


def local(vectors, gauge_x, gauge_y):
    ngx, nyz = lax.axis_size("gx"), lax.axis_size("yz")
    _, _, nx, ny, nz, nv = vectors.shape
    chips = ngx // 2 * nyz
    scaling = 1.0 / math.sqrt(3.0 * nx * ngx * ny * nyz * nz)
    sites = 3 * nx * ny * nz
    out = pl.pallas_call(
        functools.partial(kernel, ngx, nyz, scaling),
        out_shape=jax.ShapeDtypeStruct((2, 2 * nv, nv), jnp.float32),
        in_specs=[pl.BlockSpec(memory_space=pl.ANY)] * 3,
        out_specs=pl.BlockSpec(memory_space=pltpu.VMEM),
        scratch_shapes=[
            pltpu.VMEM((2, 3, nx + 1, ny, nz, nv), jnp.bfloat16),
            pltpu.VMEM((2, 3, nx, nz, nv), jnp.bfloat16),
            pltpu.VMEM((2,) + gauge_x.shape, jnp.float32),
            pltpu.VMEM((nx, 2 * nv, 3 * ny * nz), jnp.bfloat16),
            pltpu.VMEM((2 * nv, 2 * nv), jnp.float32),
            pltpu.VMEM((2, 2 * nv, nv), jnp.float32),
            pltpu.VMEM((2, nv, nv), jnp.float32),
            pltpu.VMEM((2, chips, nv // chips, nv), jnp.float32),
            pltpu.SemaphoreType.DMA((nx,)),
            pltpu.SemaphoreType.DMA((2,)),
            pltpu.SemaphoreType.DMA((2,)),
            pltpu.SemaphoreType.DMA((2,)),
            pltpu.SemaphoreType.DMA((2,)),
            pltpu.SemaphoreType.DMA((2,)),
            pltpu.SemaphoreType.DMA((2, chips)),
            pltpu.SemaphoreType.DMA((2, chips)),
            pltpu.SemaphoreType.DMA((2, chips)),
            pltpu.SemaphoreType.DMA((2, chips)),
            pltpu.SemaphoreType.DMA((2, chips)),
            pltpu.SemaphoreType.DMA((2, chips)),
        ],
        compiler_params=pltpu.CompilerParams(
            collective_id=0, has_side_effects=True, vmem_limit_bytes=int(53.3 * 1024 * 1024)
        ),
        cost_estimate=pl.CostEstimate(
            flops=24 * sites * nv * nv, bytes_accessed=4 * sites * nv, transcendentals=0
        ),
        name="elementals",
    )(vectors, gauge_x, gauge_y)
    return out.reshape(2, 2, nv, nv)


def solution(mesh):
    placed = (
        P(None, None, "gx", "yz", "ta", None),
        P(None, None, None, "gx", "yz", "ta"),
        P(None, None, None, "gx", "yz", "ta"),
    )
    return jax.shard_map(
        local, mesh=mesh, in_specs=placed, out_specs=P("ta", None, None, None), check_vma=False
    )
```
